32 devices in a mesh: groups: 2 (over x), tensor: 16 (over z, y, core).
Axes of the slice: x: 2, y: 2, z: 4, core: 2. Of those that a mesh axis runs over, the one named last changes fastest.
Arguments:
- tokens: bfloat16 [768, 8192], P(('groups', 'tensor')), parts along dimension 0, may hold values from -6 to 6
- gate_weight: bfloat16 [8192, 14336], P(None, 'tensor'), may hold values from -0.0625 to 0.0625
- up_weight: bfloat16 [8192, 14336], P(None, 'tensor'), may hold values from -0.0625 to 0.0625
- down_weight: bfloat16 [14336, 8192], P('tensor'), may hold values from -0.046875 to 0.046875
- adapter_shrink: bfloat16 [16, 64, 8192], P('tensor'), may hold values from -0.0625 to 0.0625
- adapter_expand: bfloat16 [16, 64, 14336], P(None, None, 'tensor'), may hold values from -0.75 to 0.75
- adapter_list: int32 [28], P('groups'), parts along dimension 0, may hold values from 0 to 15, as said below
- block_slot: int32 [48], P('groups'), parts along dimension 0, may hold values from 0 to 13, never falling along the last dimension, each value on 1 to 6 neighbouring positions
- pool_slot: int32 [16], replicated, may hold values from 0 to 15, each once
Outputs:
- mixed: bfloat16 [768, 8192], P(('groups', 'tensor')), parts along dimension 0
The draws below stay inside these ranges and needn't reach their ends.
There are 2 independent parts, one for each index of `groups`. The reference program is written for one: setup_inputs(seed, part) draws one part's arguments, and reference() takes and returns one part's arrays. A program takes and returns all parts, laid end to end along the dimension named above; an argument that names none is the same for every part. Nothing has to cross between parts.
Inputs may be any that keep to these rules, and one draw needn't show every extreme that they name: `adapter_list`: 14 distinct adapter ids. `block_slot`: never falls from block to block; every entry of the list has 1 to 6 blocks, one exactly 6. `pool_slot`: a permutation; pool row p lies on the device of tensor index p.
All inputs are finite; a program needn't handle non-finite values.
Results may differ from the reference program's by a relative error of at most 0.014.
Values may be sent and summed in bfloat16 or wider, within the bound.
A program may use at most 128 MiB of HBM per device.

```python
import math
import jax
import jax.numpy as jnp
import numpy as np
from jax import lax

D = 8192
FFW = 14336
R = 64
BLK = 16
NEED = 14
ADAPTERS = 16
GROUP_TOKENS = 384
BLOCKS = 24
N_TENSOR = 16


def draw_adapter_list(key, part):
    key = jax.random.fold_in(key, 11)
    return jax.random.permutation(key, ADAPTERS)[:NEED].astype(jnp.int32)


def level_of(own_key, dims, shards, smallest, high):
    def one(axis_at, parts):
        steps = jax.random.uniform(jax.random.fold_in(jax.random.fold_in(own_key, 6), axis_at), (parts,), jnp.float32, smallest / len(shards), high / len(shards))
        return jnp.repeat(jnp.exp(steps), dims[axis_at] // parts).reshape((-1,) + (1,) * (len(dims) - axis_at - 1))

    loudness = one(*shards[0])
    for cut in shards[1:]:
        loudness = loudness * one(*cut)
    return loudness


def profile(amount, total, most, skew):
    loads = [(1 << 20) // math.isqrt(grade ** skew) + 1 for grade in range(2, amount + 1)]
    spare, holding = total - most - (amount - 1), [1] * (amount - 1)
    while spare > 0:
        free = [i for i in range(amount - 1) if holding[i] < most]
        pool, remaining = sum([loads[i] for i in free]), spare
        for i in free:
            more = min(most - holding[i], max(1, remaining * loads[i] // pool), spare)
            holding[i] = holding[i] + more
            spare = spare - more
    return np.array([most] + holding)


def uneven_parts(key, number_of, total, bound, lean):
    if number_of == 2:
        one = jax.random.randint(key, (), max(1, total - bound), min(bound, total - 1) + 1)
        return jnp.stack([one, total - one])
    sizes = jnp.asarray(profile(number_of, total, bound, lean), jnp.int32)
    pairs = (number_of - 1) // 2
    source_of, receiver = sizes[1:1 + 2 * pairs:2], sizes[2:2 + 2 * pairs:2]
    slack = jnp.minimum(source_of - 1, bound - receiver)
    passed = jax.random.randint(jax.random.fold_in(key, 1), (pairs,), 0, 1 << 20) % (slack + 1)
    sizes = sizes.at[1:1 + 2 * pairs:2].set(source_of - passed).at[2:2 + 2 * pairs:2].set(receiver + passed)
    return sizes[jax.random.permutation(jax.random.fold_in(key, 2), number_of)]


def noise(rng, shape, width, reach, split=(), dtype=jnp.bfloat16):
    factor_of = level_of(rng, shape, split, -0.22, 0.18) if split else 1.0
    drawn = jax.random.normal(rng, shape, jnp.float32) * width * factor_of
    return jnp.minimum(jnp.maximum(drawn, -reach), reach).astype(dtype)


def setup_inputs(seed: int = 0, part: int = 0) -> dict:
    keys = jax.random.split(jax.random.key(seed), 10)
    part_keys = jax.random.split(jax.random.fold_in(keys[9], part), 10)
    return {
        "tokens": noise(part_keys[0], (GROUP_TOKENS, D), 1.0, 6.0, ((0, 16),)),
        "gate_weight": noise(keys[1], (D, FFW), D ** -0.5, 0.0625, ((1, 16),)),
        "up_weight": noise(keys[2], (D, FFW), D ** -0.5, 0.0625, ((1, 16),)),
        "down_weight": noise(keys[3], (FFW, D), FFW ** -0.5, 0.046875, ((0, 16),)),
        "adapter_shrink": noise(keys[4], (ADAPTERS, R, D), D ** -0.5, 0.0625, ((0, 16),)),
        "adapter_expand": noise(keys[5], (ADAPTERS, R, FFW), R ** -0.5, 0.75, ((2, 16),)),
        "adapter_list": draw_adapter_list(jax.random.fold_in(jax.random.fold_in(keys[9], part), 71), part),
        "block_slot": jnp.searchsorted(jnp.cumsum(uneven_parts(part_keys[7], NEED, BLOCKS, BLOCKS // 4, 2)), jnp.arange(BLOCKS), side="right").astype(jnp.int32),
        "pool_slot": jax.random.permutation(keys[8], ADAPTERS).astype(jnp.int32),
    }


def reference(tokens, gate_weight, up_weight, down_weight, adapter_shrink, adapter_expand, adapter_list, block_slot, pool_slot):
    token_count = tokens.shape[0]
    count_of_blocks = token_count // BLK
    block_adapter = adapter_list[block_slot]
    shrink_tiles = adapter_shrink[pool_slot[block_adapter]].astype(jnp.float32)
    blocks_of_tokens = tokens.reshape(count_of_blocks, BLK, D).astype(jnp.float32)
    reduced_rank_output = jnp.einsum("txz,taz->txa", blocks_of_tokens, shrink_tiles).astype(jnp.bfloat16)
    expand_panels = adapter_expand[block_adapter].astype(jnp.float32)
    adapted = jnp.einsum("bkr,brf->bkf", reduced_rank_output.astype(jnp.float32), expand_panels).reshape(token_count, FFW)
    gate = jnp.dot(tokens, gate_weight, preferred_element_type=jnp.float32)
    up = jnp.dot(tokens, up_weight, preferred_element_type=jnp.float32) + adapted
    hidden = (jax.nn.silu(gate) * up).astype(jnp.bfloat16)
    slice_width = FFW // N_TENSOR
    hidden_groups = jnp.transpose(hidden.reshape(token_count, N_TENSOR, slice_width), (1, 0, 2))
    down_groups = down_weight.reshape(N_TENSOR, slice_width, D)

    def add_group(running, shard_pair):
        partial_sum = jnp.dot(shard_pair[0], shard_pair[1], preferred_element_type=jnp.float32).astype(jnp.bfloat16)
        partial_sum = lax.optimization_barrier(partial_sum)
        return running + partial_sum.astype(jnp.float32), None

    running, _ = lax.scan(add_group, jnp.zeros((token_count, D), jnp.float32), (hidden_groups, down_groups))
    return running.astype(jnp.bfloat16)
```

```python
import functools
import jax
import jax.numpy as jnp
from jax import lax
from jax.experimental import pallas as pl
from jax.experimental.pallas import tpu as pltpu
from jax.sharding import PartitionSpec as P

MESH = pl.DeviceIdType.MESH
PH = 4
SUB = 2
F32 = jnp.float32
BF16 = jnp.bfloat16


def dot(a, b):
    return jnp.dot(a, b, preferred_element_type=F32)


def spans(width, unit):
    return [(lo, min(unit, width - lo)) for lo in range(0, width, unit)]


def kernel(
    fold,
    x_in,
    wg_hbm,
    wu_hbm,
    wd_hbm,
    shrink_hbm,
    expand_hbm,
    own_mask_hbm,
    row_pair_hbm,
    out,
    x,
    wg,
    wu,
    wd,
    s2,
    ex,
    own_mask,
    row_pair,
    accg,
    accu,
    accs,
    hid,
    sib,
    ring,
    ar_out,
    ar_in,
    load_sem,
    w_sem,
    s_sem,
    d_sem,
    m_sem,
    ag_send,
    ag_recv,
    fw_send,
    fw_recv,
    ar_send,
    ar_recv,
    sx_send,
    sx_recv,
    rs_send,
    rs_recv,
):
    rows = x_in.shape[0]
    n = x.shape[2] // rows
    width = x.shape[3]
    part = width // SUB
    half = PH * width
    ffw = wg.shape[3]
    stages = ar_out.shape[0]
    group = lax.axis_index("groups")
    me = lax.axis_index("tensor")
    core = me % 2
    chip = me // 2
    way = 1 - 2 * core
    if fold:
        zz, yy = chip // 2, chip % 2
        pos = yy * (n - 1 - zz) + (1 - yy) * zz
    else:
        pos = chip

    def chip_at(p):
        p = (p + 2 * n) % n
        if fold:
            up = p // (n // 2)
            return up * (2 * (n - 1 - p) + 1) + (1 - up) * 2 * p
        return p

    nxt = chip_at(pos + way) * 2 + core
    prv = chip_at(pos - way) * 2 + core
    other = me + way
    partners = [me + (1 - 2 * ((me // (1 << b)) % 2)) * (1 << b) for b in range(stages)]

    def rows_of(step):
        return pl.ds(pl.multiple_of(chip_at(pos - way * step) * rows, 16), rows)

    def load(ph):
        return pltpu.make_async_copy(
            x_in.at[:, pl.ds(pl.multiple_of(ph * width, 128), width)],
            x.at[core, ph, rows_of(0), :],
            load_sem.at[ph],
        )

    def ag(ph, m, step):
        ref = x.at[core, ph, rows_of(step), pl.ds(m * part, part)]
        return pltpu.make_async_remote_copy(
            src_ref=ref, dst_ref=ref, send_sem=ag_send.at[ph, m, step], recv_sem=ag_recv.at[ph, m, step],
            device_id=(group, nxt), device_id_type=MESH,
        )

    def fw(ph, m, step):
        ref = x.at[core, ph, rows_of(step), pl.ds(m * part, part)]
        return pltpu.make_async_remote_copy(
            src_ref=ref, dst_ref=ref, send_sem=fw_send.at[ph, m, step], recv_sem=fw_recv.at[ph, m, step],
            device_id=(group, other), device_id_type=MESH,
        )

    def w_copies(ph):
        return [
            pltpu.make_async_copy(src.at[h, ph], dst.at[h, ph], w_sem.at[i, h, ph])
            for h in range(2)
            for i, (src, dst) in enumerate(((wg_hbm, wg), (wu_hbm, wu)))
        ]

    def s_copies(ph):
        rank = shrink_hbm.shape[0]
        return [
            pltpu.make_async_copy(
                shrink_hbm.at[:, pl.ds(pl.multiple_of(h * half + ph * width, 128), width)],
                s2.at[h, ph, pl.ds(i * rank, rank), :],
                s_sem.at[i, h, ph],
            )
            for h in range(2)
            for i in range(2)
        ]

    def d_copy(h, ph):
        return pltpu.make_async_copy(
            wd_hbm.at[:, pl.ds(pl.multiple_of(h * half + ph * width, 128), width)], wd.at[h, ph], d_sem.at[h, ph]
        )

    m_copies = [
        pltpu.make_async_copy(src, dst, m_sem.at[i])
        for i, (src, dst) in enumerate(((expand_hbm, ex), (own_mask_hbm, own_mask), (row_pair_hbm, row_pair)))
    ]

    for ph in range(PH):
        load(ph).start()
    barrier = pltpu.get_barrier_semaphore()
    greet = [nxt, prv] + partners
    for dev in greet:
        pl.semaphore_signal(barrier, inc=1, device_id=(group, dev), device_id_type=MESH)
    pl.semaphore_wait(barrier, len(greet))

    def begin(ph):
        load(ph).wait()
        for m in range(SUB):
            ag(ph, m, 0).start()
            fw(ph, m, 0).start()

    begin(0)
    for ph in range(PH):
        for cp in w_copies(ph) + s_copies(ph):
            cp.start()
    for cp in m_copies:
        cp.start()
    for ph in range(PH):
        for h in range(2):
            d_copy(h, ph).start()
    accg[...] = jnp.zeros_like(accg)
    accu[...] = jnp.zeros_like(accu)
    accs[...] = jnp.zeros_like(accs)

    def ready(ph):
        def one(step, _):
            for m in range(SUB):
                fw(ph, m, step).wait_recv()
            return 0

        lax.fori_loop(0, n, one, 0)
        for cp in w_copies(ph) + s_copies(ph):
            cp.wait()

    def shrink_unit(ph):
        for h in range(2):
            accs[...] += lax.dot_general(
                x[h, ph], s2[h, ph], (((1,), (1,)), ((), ())), preferred_element_type=F32
            )

    def unit(ph, acc, w, lo, size):
        acc[:, lo : lo + size] += dot(x[0, ph], w[0, ph, :, lo : lo + size]) + dot(
            x[1, ph], w[1, ph, :, lo : lo + size]
        )

    units = [(acc, w, lo, size) for lo, size in spans(ffw, 256) for acc, w in ((accg, wg), (accu, wu))]
    share = -(-len(units) // (n - 1))

    def phase(ph, _):
        for step in range(1, n):
            if step == n - 1:

                @pl.when(ph + 1 < PH)
                def _():
                    begin(ph + 1)

            for m in range(SUB):
                ag(ph, m, step - 1).wait_recv()
                if step < n - 1:
                    ag(ph, m, step).start()
                fw(ph, m, step).start()

            mine = units[(step - 1) * share : step * share]
            if mine or step == 1:

                @pl.when(ph > 0)
                def _(mine=mine, step=step):
                    if step == 1:
                        ready(ph - 1)
                        shrink_unit(ph - 1)
                    for u in mine:
                        unit(ph - 1, *u)

        return 0

    lax.fori_loop(0, PH, phase, 0)

    last = PH - 1
    ready(last)
    shrink_unit(last)
    for cp in m_copies:
        cp.wait()
    owned = accs[...] * own_mask[...].astype(F32)
    tall = owned.shape[0] // 2
    packed = (owned[:tall] + owned[tall:]).astype(BF16)
    share = -(-len(units) // stages)
    for b in range(stages):
        ar_out[b] = packed
        cp = pltpu.make_async_remote_copy(
            src_ref=ar_out.at[b], dst_ref=ar_in.at[b], send_sem=ar_send.at[b], recv_sem=ar_recv.at[b],
            device_id=(group, partners[b]), device_id_type=MESH,
        )
        cp.start()
        for u in units[b * share : (b + 1) * share]:
            unit(last, *u)
        cp.wait()
        packed = (ar_out[b].astype(F32) + ar_in[b].astype(F32)).astype(BF16)

    rank = packed.shape[1] // 2
    whole = packed.astype(F32)
    turned = pltpu.roll(whole, rank, 1)
    low = lax.broadcasted_iota(jnp.int32, whole.shape, 1) < rank
    twice = jnp.concatenate([jnp.where(low, whole, turned), jnp.where(low, turned, whole)], axis=0).astype(BF16)

    def drain(ph, _):
        def one(step, _):
            for m in range(SUB):
                fw(ph, m, step).wait_send()
            return 0

        lax.fori_loop(0, n, one, 0)

        def two(step, _):
            for m in range(SUB):
                ag(ph, m, step).wait_send()
            return 0

        lax.fori_loop(0, n - 1, two, 0)
        return 0

    lax.fori_loop(0, PH, drain, 0)

    twice32 = twice.astype(F32)
    pair_of = row_pair[...].astype(F32)
    taken = ex.shape[0] // width
    for k in range(ex.shape[0] // (2 * rank)):
        lo = k * 2 * rank
        x[0, lo // width, :, lo % width : lo % width + 2 * rank] = jnp.where(pair_of == 2.0 * k, twice32, 0.0).astype(BF16)
    for lo, size in spans(ffw, 256):
        gate = accg[:, lo : lo + size]
        up = accu[:, lo : lo + size]
        for k in range(taken):
            up += dot(x[0, k], ex[k * width : (k + 1) * width, lo : lo + size])
        hid[:, lo : lo + size] = (gate / (1.0 + jnp.exp(-gate)) * up).astype(BF16)

    def sx(c):
        return pltpu.make_async_remote_copy(
            src_ref=x.at[1 - core, c], dst_ref=sib.at[c], send_sem=sx_send.at[c], recv_sem=sx_recv.at[c],
            device_id=(group, other), device_id_type=MESH,
        )

    def rs(c, step):
        return pltpu.make_async_remote_copy(
            src_ref=x.at[core, c, rows_of(step + 1), :], dst_ref=ring.at[c, step],
            send_sem=rs_send.at[c, step], recv_sem=rs_recv.at[c, step],
            device_id=(group, nxt), device_id_type=MESH,
        )

    def down(c):
        def fill(h):
            d_copy(h, c).wait()
            for lo, size in spans(width, 256):
                x[h, c, :, lo : lo + size] = dot(hid[...], wd[h, c, :, lo : lo + size]).astype(BF16)

        fill(1 - core)
        sx(c).start()
        fill(core)

    def slot(t, _):
        @pl.when(t < PH)
        def _():
            down(t)

        for c in range(PH):
            step = t - c

            @pl.when(step == 0)
            def _(c=c):
                sx(c).wait_recv()
                r = rows_of(1)
                x[core, c, r, :] = (x[core, c, r, :].astype(F32) + sib[c, r, :].astype(F32)).astype(BF16)
                rs(c, 0).start()

            @pl.when(jnp.logical_and(step > 0, step < n))
            def _(c=c, step=step):
                rs(c, step - 1).wait_recv()
                r = rows_of(step + 1)
                total = (
                    x[core, c, r, :].astype(F32) + sib[c, r, :].astype(F32) + ring[c, step - 1].astype(F32)
                ).astype(BF16)

                @pl.when(step < n - 1)
                def _():
                    x[core, c, r, :] = total
                    rs(c, step).start()

                @pl.when(step == n - 1)
                def _():
                    out[:, c * width : (c + 1) * width] = total

        return 0

    lax.fori_loop(0, n + PH - 1, slot, 0)
    for c in range(PH):
        sx(c).wait_send()

        def three(step, _, c=c):
            rs(c, step).wait_send()
            return 0

        lax.fori_loop(0, n - 1, three, 0)


def local(count, tokens, gate_weight, up_weight, down_weight, adapter_shrink, adapter_expand, adapter_list, block_slot, pool_slot):
    own_rows, model = tokens.shape
    half = model // 2
    width = half // PH
    n = count // 2
    rows = 2 * own_rows
    token_count = n * rows
    rank = adapter_shrink.shape[1]
    ffw = gate_weight.shape[1]
    adapters = adapter_expand.shape[0]
    stages = count.bit_length() - 1
    me = lax.axis_index("tensor")
    core = me % 2
    swap = [(i, i ^ 1) for i in range(count)]

    kept = lax.dynamic_slice_in_dim(tokens, core * half, half, 1)
    given = lax.dynamic_slice_in_dim(tokens, (1 - core) * half, half, 1)
    got = lax.ppermute(given, "tensor", swap)
    x_in = jnp.where(core == 0, jnp.concatenate([kept, got]), jnp.concatenate([got, kept]))

    block_adapter = adapter_list[block_slot]
    block_rows = token_count // block_slot.shape[0]
    row_adapter = jnp.repeat(block_adapter, block_rows, total_repeat_length=token_count)
    row_pool = jnp.repeat(pool_slot[block_adapter], block_rows, total_repeat_length=token_count)
    second = jnp.arange(token_count) >= token_count // 2
    lane = jnp.arange(2 * rank) >= rank
    own_mask = jnp.logical_and((row_pool == me)[:, None], second[:, None] == lane[None, :]).astype(BF16)
    row_pair = (row_adapter[:, None] - lane[None, :].astype(jnp.int32)).astype(BF16)

    dma = pltpu.SemaphoreType.DMA
    flops = 2 * token_count * model * ffw * 3
    reduced = pl.pallas_call(
        functools.partial(kernel, count == 16),
        out_shape=jax.ShapeDtypeStruct((rows, half), BF16),
        in_specs=[pl.BlockSpec(memory_space=pl.ANY)] * 8,
        out_specs=pl.BlockSpec(memory_space=pltpu.VMEM),
        scratch_shapes=[
            pltpu.VMEM((2, PH, token_count, width), BF16),
            pltpu.VMEM((2, PH, width, ffw), BF16),
            pltpu.VMEM((2, PH, width, ffw), BF16),
            pltpu.VMEM((2, PH, ffw, width), BF16),
            pltpu.VMEM((2, PH, 2 * rank, width), BF16),
            pltpu.VMEM((adapters * rank, ffw), BF16),
            pltpu.VMEM((token_count, 2 * rank), BF16),
            pltpu.VMEM((token_count, 2 * rank), BF16),
            pltpu.VMEM((token_count, ffw), F32),
            pltpu.VMEM((token_count, ffw), F32),
            pltpu.VMEM((token_count, 2 * rank), F32),
            pltpu.VMEM((token_count, ffw), BF16),
            pltpu.VMEM((PH, token_count, width), BF16),
            pltpu.VMEM((PH, n - 1, rows, width), BF16),
            pltpu.VMEM((stages, token_count // 2, 2 * rank), BF16),
            pltpu.VMEM((stages, token_count // 2, 2 * rank), BF16),
            dma((PH,)),
            dma((2, 2, PH)),
            dma((2, 2, PH)),
            dma((2, PH)),
            dma((3,)),
            dma((PH, SUB, n - 1)),
            dma((PH, SUB, n - 1)),
            dma((PH, SUB, n)),
            dma((PH, SUB, n)),
            dma((stages,)),
            dma((stages,)),
            dma((PH,)),
            dma((PH,)),
            dma((PH, n - 1)),
            dma((PH, n - 1)),
        ],
        compiler_params=pltpu.CompilerParams(
            collective_id=0, has_side_effects=True, vmem_limit_bytes=63 * 1024 * 1024
        ),
        cost_estimate=pl.CostEstimate(flops=flops, bytes_accessed=6 * model * ffw, transcendentals=token_count * ffw),
    )(
        x_in,
        gate_weight.reshape(2, PH, width, ffw),
        up_weight.reshape(2, PH, width, ffw),
        down_weight,
        adapter_shrink[0],
        adapter_expand.reshape(adapters * rank, ffw),
        own_mask,
        row_pair,
    )
    mine = lax.dynamic_slice_in_dim(reduced, core * own_rows, own_rows, 0)
    theirs = lax.dynamic_slice_in_dim(reduced, (1 - core) * own_rows, own_rows, 0)
    got = lax.ppermute(theirs, "tensor", swap)
    return jnp.where(core == 0, jnp.concatenate([mine, got], 1), jnp.concatenate([got, mine], 1))


def solution(mesh):
    return jax.shard_map(
        functools.partial(local, mesh.shape["tensor"]),
        mesh=mesh,
        in_specs=(
            P(("groups", "tensor"), None),
            P(None, "tensor"),
            P(None, "tensor"),
            P("tensor", None),
            P("tensor", None, None),
            P(None, None, "tensor"),
            P("groups"),
            P("groups"),
            P(),
        ),
        out_specs=P(("groups", "tensor"), None),
        check_vma=False,
    )
```

```python
import functools
import jax
import jax.numpy as jnp
from jax import lax
from jax.experimental import pallas as pl
from jax.experimental.pallas import tpu as pltpu
from jax.sharding import PartitionSpec as P

MESH = pl.DeviceIdType.MESH
PH = 4
SUB = 1
F32 = jnp.float32
BF16 = jnp.bfloat16


def dot(a, b):
    return jnp.dot(a, b, preferred_element_type=F32)


def spans(width, unit):
    return [(lo, min(unit, width - lo)) for lo in range(0, width, unit)]


def kernel(
    fold,
    x_in,
    wg_hbm,
    wu_hbm,
    wd_hbm,
    shrink_hbm,
    expand_hbm,
    adapter_list,
    block_slot,
    pool_slot,
    out,
    x,
    wg,
    wu,
    wd,
    s2,
    ex,
    own_mask,
    row_pair,
    accg,
    accu,
    accs,
    hid,
    sib,
    ring,
    ar_out,
    ar_in,
    load_sem,
    w_sem,
    s_sem,
    d_sem,
    m_sem,
    ag_send,
    ag_recv,
    fw_send,
    fw_recv,
    ar_send,
    ar_recv,
    sx_send,
    sx_recv,
    rs_send,
    rs_recv,
):
    rows = x_in.shape[0]
    n = x.shape[2] // rows
    width = x.shape[3]
    part = width // SUB
    half = PH * width
    ffw = wg.shape[3]
    stages = ar_out.shape[0]
    group = lax.axis_index("groups")
    me = lax.axis_index("tensor")
    core = me % 2
    chip = me // 2
    way = 1 - 2 * core
    if fold:
        zz, yy = chip // 2, chip % 2
        pos = yy * (n - 1 - zz) + (1 - yy) * zz
    else:
        pos = chip

    def chip_at(p):
        p = (p + 2 * n) % n
        if fold:
            up = p // (n // 2)
            return up * (2 * (n - 1 - p) + 1) + (1 - up) * 2 * p
        return p

    nxt = chip_at(pos + way) * 2 + core
    prv = chip_at(pos - way) * 2 + core
    other = me + way
    partners = [me + (1 - 2 * ((me // (1 << b)) % 2)) * (1 << b) for b in range(stages)]

    def rows_of(step):
        return pl.ds(pl.multiple_of(chip_at(pos - way * step) * rows, 16), rows)

    def load(ph):
        return pltpu.make_async_copy(
            x_in.at[:, pl.ds(pl.multiple_of(ph * width, 128), width)],
            x.at[core, ph, rows_of(0), :],
            load_sem.at[ph],
        )

    def ag(ph, m, step):
        ref = x.at[core, ph, rows_of(step), pl.ds(m * part, part)]
        return pltpu.make_async_remote_copy(
            src_ref=ref, dst_ref=ref, send_sem=ag_send.at[ph, m, step], recv_sem=ag_recv.at[ph, m, step],
            device_id=(group, nxt), device_id_type=MESH,
        )

    def fw(ph, m, step):
        ref = x.at[core, ph, rows_of(step), pl.ds(m * part, part)]
        return pltpu.make_async_remote_copy(
            src_ref=ref, dst_ref=ref, send_sem=fw_send.at[ph, m, step], recv_sem=fw_recv.at[ph, m, step],
            device_id=(group, other), device_id_type=MESH,
        )

    def w_copies(ph):
        return [
            pltpu.make_async_copy(src.at[h, ph], dst.at[h, ph], w_sem.at[i, h, ph])
            for h in range(2)
            for i, (src, dst) in enumerate(((wg_hbm, wg), (wu_hbm, wu)))
        ]

    def s_copies(ph):
        rank = shrink_hbm.shape[0]
        return [
            pltpu.make_async_copy(
                shrink_hbm.at[:, pl.ds(pl.multiple_of(h * half + ph * width, 128), width)],
                s2.at[h, ph, pl.ds(i * rank, rank), :],
                s_sem.at[i, h, ph],
            )
            for h in range(2)
            for i in range(2)
        ]

    def d_copy(h, ph):
        return pltpu.make_async_copy(
            wd_hbm.at[:, pl.ds(pl.multiple_of(h * half + ph * width, 128), width)], wd.at[h, ph], d_sem.at[h, ph]
        )

    m_copies = [pltpu.make_async_copy(expand_hbm, ex, m_sem.at[0])]

    for ph in range(PH):
        load(ph).start()
    barrier = pltpu.get_barrier_semaphore()
    greet = [nxt, prv] + partners
    for dev in greet:
        pl.semaphore_signal(barrier, inc=1, device_id=(group, dev), device_id_type=MESH)
    pl.semaphore_wait(barrier, len(greet))

    def begin(ph):
        load(ph).wait()
        for m in range(SUB):
            ag(ph, m, 0).start()
            fw(ph, m, 0).start()

    for ph in range(PH):
        for cp in w_copies(ph) + s_copies(ph):
            cp.start()
    for cp in m_copies:
        cp.start()
    for ph in range(PH):
        for h in range(2):
            d_copy(h, ph).start()
    accg[...] = jnp.zeros_like(accg)
    accu[...] = jnp.zeros_like(accu)
    accs[...] = jnp.zeros_like(accs)
    blocks = block_slot.shape[0]
    block_rows = own_mask.shape[0] // blocks
    upper = (lax.broadcasted_iota(jnp.int32, (block_rows, own_mask.shape[1]), 1) >= own_mask.shape[1] // 2).astype(F32)

    def marks(b, _):
        adapter = adapter_list[block_slot[b]]
        here = (pool_slot[adapter] == me).astype(F32)
        second = (b >= blocks // 2).astype(F32)
        at = pl.ds(pl.multiple_of(b * block_rows, 16), block_rows)
        own_mask[at, :] = here * (1.0 - jnp.abs(upper - second))
        row_pair[at, :] = adapter.astype(F32) - upper
        return 0

    lax.fori_loop(0, blocks, marks, 0)

    def ready(ph):
        def one(step, _):
            for m in range(SUB):
                fw(ph, m, step).wait_recv()
            return 0

        lax.fori_loop(0, n, one, 0)
        for cp in w_copies(ph) + s_copies(ph):
            cp.wait()

    def shrink_unit(ph):
        for h in range(2):
            accs[...] += lax.dot_general(
                x[h, ph], s2[h, ph], (((1,), (1,)), ((), ())), preferred_element_type=F32
            )

    def unit(ph, acc, w, lo, size):
        acc[:, lo : lo + size] += dot(x[0, ph], w[0, ph, :, lo : lo + size]) + dot(
            x[1, ph], w[1, ph, :, lo : lo + size]
        )

    units = [(acc, w, lo, size) for lo, size in spans(ffw, 256) for acc, w in ((accg, wg), (accu, wu))]
    def wave(t, _):
        for c in range(PH):
            step = t - c

            @pl.when(step == 0)
            def _(c=c):
                begin(c)

            @pl.when(jnp.logical_and(step > 0, step < n))
            def _(c=c, step=step):
                for m in range(SUB):
                    ag(c, m, step - 1).wait_recv()

                    @pl.when(step < n - 1)
                    def _(m=m):
                        ag(c, m, step).start()

                    fw(c, m, step).start()

        @pl.when(t >= n)
        def _():
            ready(t - n)
            shrink_unit(t - n)
            for u in units:
                unit(t - n, *u)

        return 0

    lax.fori_loop(0, n + PH - 1, wave, 0)

    last = PH - 1
    ready(last)
    shrink_unit(last)
    for cp in m_copies:
        cp.wait()
    owned = accs[...] * own_mask[...]
    tall = owned.shape[0] // 2
    packed = (owned[:tall] + owned[tall:]).astype(BF16)
    share = -(-len(units) // stages)
    for b in range(stages):
        ar_out[b] = packed
        cp = pltpu.make_async_remote_copy(
            src_ref=ar_out.at[b], dst_ref=ar_in.at[b], send_sem=ar_send.at[b], recv_sem=ar_recv.at[b],
            device_id=(group, partners[b]), device_id_type=MESH,
        )
        cp.start()
        for u in units[b * share : (b + 1) * share]:
            unit(last, *u)
        cp.wait()
        packed = (ar_out[b].astype(F32) + ar_in[b].astype(F32)).astype(BF16)

    rank = packed.shape[1] // 2
    whole = packed.astype(F32)
    turned = pltpu.roll(whole, rank, 1)
    low = lax.broadcasted_iota(jnp.int32, whole.shape, 1) < rank
    twice = jnp.concatenate([jnp.where(low, whole, turned), jnp.where(low, turned, whole)], axis=0).astype(BF16)

    def drain(ph, _):
        def one(step, _):
            for m in range(SUB):
                fw(ph, m, step).wait_send()
            return 0

        lax.fori_loop(0, n, one, 0)

        def two(step, _):
            for m in range(SUB):
                ag(ph, m, step).wait_send()
            return 0

        lax.fori_loop(0, n - 1, two, 0)
        return 0

    lax.fori_loop(0, PH, drain, 0)

    twice32 = twice.astype(F32)
    pair_of = row_pair[...]
    taken = ex.shape[0] // width
    for k in range(ex.shape[0] // (2 * rank)):
        lo = k * 2 * rank
        x[0, lo // width, :, lo % width : lo % width + 2 * rank] = jnp.where(pair_of == 2.0 * k, twice32, 0.0).astype(BF16)
    for lo, size in spans(ffw, 256):
        gate = accg[:, lo : lo + size]
        up = accu[:, lo : lo + size]
        for k in range(taken):
            up += dot(x[0, k], ex[k * width : (k + 1) * width, lo : lo + size])
        hid[:, lo : lo + size] = (gate / (1.0 + jnp.exp(-gate)) * up).astype(BF16)

    def sx(c):
        return pltpu.make_async_remote_copy(
            src_ref=x.at[1 - core, c], dst_ref=sib.at[c], send_sem=sx_send.at[c], recv_sem=sx_recv.at[c],
            device_id=(group, other), device_id_type=MESH,
        )

    def rs(c, step):
        return pltpu.make_async_remote_copy(
            src_ref=x.at[core, c, rows_of(step + 1), :], dst_ref=ring.at[c, step],
            send_sem=rs_send.at[c, step], recv_sem=rs_recv.at[c, step],
            device_id=(group, nxt), device_id_type=MESH,
        )

    def down(c):
        def fill(h):
            d_copy(h, c).wait()
            for lo, size in spans(width, 256):
                x[h, c, :, lo : lo + size] = dot(hid[...], wd[h, c, :, lo : lo + size]).astype(BF16)

        fill(1 - core)
        sx(c).start()
        fill(core)

    def kick(c):
        sx(c).wait_recv()
        r = rows_of(1)
        x[core, c, r, :] = (x[core, c, r, :].astype(F32) + sib[c, r, :].astype(F32)).astype(BF16)
        rs(c, 0).start()

    def lead(c, _):
        down(c)

        @pl.when(c > 0)
        def _():
            kick(c - 1)

        return 0

    lax.fori_loop(0, PH, lead, 0)
    kick(PH - 1)

    def total(c, step):
        rs(c, step - 1).wait_recv()
        r = rows_of(step + 1)
        return (x[core, c, r, :].astype(F32) + sib[c, r, :].astype(F32) + ring[c, step - 1].astype(F32)).astype(BF16)

    def hop(step, _):
        for c in range(PH):
            x[core, c, rows_of(step + 1), :] = total(c, step)
            rs(c, step).start()
        return 0

    lax.fori_loop(1, n - 1, hop, 0)
    for c in range(PH):
        out[:, c * width : (c + 1) * width] = total(c, n - 1)
    for c in range(PH):
        sx(c).wait_send()

        def three(step, _, c=c):
            rs(c, step).wait_send()
            return 0

        lax.fori_loop(0, n - 1, three, 0)


def local(count, tokens, gate_weight, up_weight, down_weight, adapter_shrink, adapter_expand, adapter_list, block_slot, pool_slot):
    own_rows, model = tokens.shape
    half = model // 2
    width = half // PH
    n = count // 2
    rows = 2 * own_rows
    token_count = n * rows
    rank = adapter_shrink.shape[1]
    ffw = gate_weight.shape[1]
    adapters = adapter_expand.shape[0]
    stages = count.bit_length() - 1
    core = lax.axis_index("tensor") % 2
    swap = [(i, i ^ 1) for i in range(count)]

    kept = lax.dynamic_slice_in_dim(tokens, core * half, half, 1)
    given = lax.dynamic_slice_in_dim(tokens, (1 - core) * half, half, 1)
    got = lax.ppermute(given, "tensor", swap)
    x_in = jnp.where(core == 0, jnp.concatenate([kept, got]), jnp.concatenate([got, kept]))

    dma = pltpu.SemaphoreType.DMA
    flops = 2 * token_count * model * ffw * 3
    reduced = pl.pallas_call(
        functools.partial(kernel, count == 16),
        out_shape=jax.ShapeDtypeStruct((rows, half), BF16),
        in_specs=[pl.BlockSpec(memory_space=pl.ANY)] * 6 + [pl.BlockSpec(memory_space=pltpu.SMEM)] * 3,
        out_specs=pl.BlockSpec(memory_space=pltpu.VMEM),
        scratch_shapes=[
            pltpu.VMEM((2, PH, token_count, width), BF16),
            pltpu.VMEM((2, PH, width, ffw), BF16),
            pltpu.VMEM((2, PH, width, ffw), BF16),
            pltpu.VMEM((2, PH, ffw, width), BF16),
            pltpu.VMEM((2, PH, 2 * rank, width), BF16),
            pltpu.VMEM((adapters * rank, ffw), BF16),
            pltpu.VMEM((token_count, 2 * rank), F32),
            pltpu.VMEM((token_count, 2 * rank), F32),
            pltpu.VMEM((token_count, ffw), F32),
            pltpu.VMEM((token_count, ffw), F32),
            pltpu.VMEM((token_count, 2 * rank), F32),
            pltpu.VMEM((token_count, ffw), BF16),
            pltpu.VMEM((PH, token_count, width), BF16),
            pltpu.VMEM((PH, n - 1, rows, width), BF16),
            pltpu.VMEM((stages, token_count // 2, 2 * rank), BF16),
            pltpu.VMEM((stages, token_count // 2, 2 * rank), BF16),
            dma((PH,)),
            dma((2, 2, PH)),
            dma((2, 2, PH)),
            dma((2, PH)),
            dma((1,)),
            dma((PH, SUB, n - 1)),
            dma((PH, SUB, n - 1)),
            dma((PH, SUB, n)),
            dma((PH, SUB, n)),
            dma((stages,)),
            dma((stages,)),
            dma((PH,)),
            dma((PH,)),
            dma((PH, n - 1)),
            dma((PH, n - 1)),
        ],
        compiler_params=pltpu.CompilerParams(
            collective_id=0, has_side_effects=True, vmem_limit_bytes=63 * 1024 * 1024
        ),
        cost_estimate=pl.CostEstimate(flops=flops, bytes_accessed=6 * model * ffw, transcendentals=token_count * ffw),
    )(
        x_in,
        gate_weight.reshape(2, PH, width, ffw),
        up_weight.reshape(2, PH, width, ffw),
        down_weight,
        adapter_shrink[0],
        adapter_expand.reshape(adapters * rank, ffw),
        adapter_list,
        block_slot,
        pool_slot,
    )
    mine = lax.dynamic_slice_in_dim(reduced, core * own_rows, own_rows, 0)
    theirs = lax.dynamic_slice_in_dim(reduced, (1 - core) * own_rows, own_rows, 0)
    got = lax.ppermute(theirs, "tensor", swap)
    return jnp.where(core == 0, jnp.concatenate([mine, got], 1), jnp.concatenate([got, mine], 1))


def solution(mesh):
    return jax.shard_map(
        functools.partial(local, mesh.shape["tensor"]),
        mesh=mesh,
        in_specs=(
            P(("groups", "tensor"), None),
            P(None, "tensor"),
            P(None, "tensor"),
            P("tensor", None),
            P("tensor", None, None),
            P(None, None, "tensor"),
            P("groups"),
            P("groups"),
            P(),
        ),
        out_specs=P(("groups", "tensor"), None),
        check_vma=False,
    )
```

```python
import functools
import jax
import jax.numpy as jnp
from jax import lax
from jax.experimental import pallas as pl
from jax.experimental.pallas import tpu as pltpu
from jax.sharding import PartitionSpec as P

MESH = pl.DeviceIdType.MESH
PH = 4
SUB = 2
F32 = jnp.float32
BF16 = jnp.bfloat16


def dot(a, b):
    return jnp.dot(a, b, preferred_element_type=F32)


def spans(width, unit):
    return [(lo, min(unit, width - lo)) for lo in range(0, width, unit)]


def kernel(
    fold,
    x_in,
    wg_hbm,
    wu_hbm,
    wd_hbm,
    shrink_hbm,
    expand_hbm,
    adapter_list,
    block_slot,
    pool_slot,
    out,
    x,
    wg,
    wu,
    wd,
    s2,
    ex,
    own_mask,
    row_pair,
    accg,
    accu,
    accs,
    hid,
    sib,
    ring,
    ar_out,
    ar_in,
    load_sem,
    w_sem,
    s_sem,
    d_sem,
    m_sem,
    ag_send,
    ag_recv,
    fw_send,
    fw_recv,
    ar_send,
    ar_recv,
    sx_send,
    sx_recv,
    rs_send,
    rs_recv,
):
    rows = x_in.shape[0]
    n = x.shape[2] // rows
    width = x.shape[3]
    part = width // SUB
    half = PH * width
    ffw = wg.shape[3]
    stages = ar_out.shape[0]
    group = lax.axis_index("groups")
    me = lax.axis_index("tensor")
    core = me % 2
    chip = me // 2
    way = 1 - 2 * core
    if fold:
        zz, yy = chip // 2, chip % 2
        pos = yy * (n - 1 - zz) + (1 - yy) * zz
    else:
        pos = chip

    def chip_at(p):
        p = (p + 2 * n) % n
        if fold:
            up = p // (n // 2)
            return up * (2 * (n - 1 - p) + 1) + (1 - up) * 2 * p
        return p

    nxt = chip_at(pos + way) * 2 + core
    prv = chip_at(pos - way) * 2 + core
    other = me + way
    partners = [me + (1 - 2 * ((me // (1 << b)) % 2)) * (1 << b) for b in range(stages)]

    def rows_of(step):
        return pl.ds(pl.multiple_of(chip_at(pos - way * step) * rows, 16), rows)

    def load(ph):
        return pltpu.make_async_copy(
            x_in.at[:, pl.ds(pl.multiple_of(ph * width, 128), width)],
            x.at[core, ph, rows_of(0), :],
            load_sem.at[ph],
        )

    def ag(ph, m, step):
        ref = x.at[core, ph, rows_of(step), pl.ds(m * part, part)]
        return pltpu.make_async_remote_copy(
            src_ref=ref, dst_ref=ref, send_sem=ag_send.at[ph, m, step], recv_sem=ag_recv.at[ph, m, step],
            device_id=(group, nxt), device_id_type=MESH,
        )

    def fw(ph, m, step):
        ref = x.at[core, ph, rows_of(step), pl.ds(m * part, part)]
        return pltpu.make_async_remote_copy(
            src_ref=ref, dst_ref=ref, send_sem=fw_send.at[ph, m, step], recv_sem=fw_recv.at[ph, m, step],
            device_id=(group, other), device_id_type=MESH,
        )

    def w_copies(ph):
        return [
            pltpu.make_async_copy(src.at[h, ph], dst.at[h, ph], w_sem.at[i, h, ph])
            for h in range(2)
            for i, (src, dst) in enumerate(((wg_hbm, wg), (wu_hbm, wu)))
        ]

    def s_copies(ph):
        rank = shrink_hbm.shape[0]
        return [
            pltpu.make_async_copy(
                shrink_hbm.at[:, pl.ds(pl.multiple_of(h * half + ph * width, 128), width)],
                s2.at[h, ph, pl.ds(i * rank, rank), :],
                s_sem.at[i, h, ph],
            )
            for h in range(2)
            for i in range(2)
        ]

    def d_copy(h, ph):
        return pltpu.make_async_copy(
            wd_hbm.at[:, pl.ds(pl.multiple_of(h * half + ph * width, 128), width)], wd.at[h, ph], d_sem.at[h, ph]
        )

    m_copies = [pltpu.make_async_copy(expand_hbm, ex, m_sem.at[0])]

    for ph in range(PH):
        load(ph).start()
    barrier = pltpu.get_barrier_semaphore()
    greet = [nxt, prv] + partners
    for dev in greet:
        pl.semaphore_signal(barrier, inc=1, device_id=(group, dev), device_id_type=MESH)
    pl.semaphore_wait(barrier, len(greet))

    def begin(ph):
        load(ph).wait()
        for m in range(SUB):
            ag(ph, m, 0).start()
            fw(ph, m, 0).start()

    for ph in range(PH):
        for cp in w_copies(ph) + s_copies(ph):
            cp.start()
    for cp in m_copies:
        cp.start()
    for ph in range(PH):
        for h in range(2):
            d_copy(h, ph).start()
    accg[...] = jnp.zeros_like(accg)
    accu[...] = jnp.zeros_like(accu)
    accs[...] = jnp.zeros_like(accs)
    blocks = block_slot.shape[0]
    block_rows = own_mask.shape[0] // blocks
    upper = (lax.broadcasted_iota(jnp.int32, (block_rows, own_mask.shape[1]), 1) >= own_mask.shape[1] // 2).astype(F32)

    def marks(b, _):
        adapter = adapter_list[block_slot[b]]
        here = (pool_slot[adapter] == me).astype(F32)
        second = (b >= blocks // 2).astype(F32)
        at = pl.ds(pl.multiple_of(b * block_rows, 16), block_rows)
        own_mask[at, :] = here * (1.0 - jnp.abs(upper - second))
        row_pair[at, :] = adapter.astype(F32) - upper
        return 0

    lax.fori_loop(0, blocks, marks, 0)

    def ready(ph):
        def one(step, _):
            for m in range(SUB):
                fw(ph, m, step).wait_recv()
            return 0

        lax.fori_loop(0, n, one, 0)
        for cp in w_copies(ph) + s_copies(ph):
            cp.wait()

    def shrink_unit(ph):
        for h in range(2):
            accs[...] += lax.dot_general(
                x[h, ph], s2[h, ph], (((1,), (1,)), ((), ())), preferred_element_type=F32
            )

    def unit(ph, acc, w, lo, size):
        acc[:, lo : lo + size] += dot(x[0, ph], w[0, ph, :, lo : lo + size]) + dot(
            x[1, ph], w[1, ph, :, lo : lo + size]
        )

    units = [(acc, w, lo, size) for lo, size in spans(ffw, 256) for acc, w in ((accg, wg), (accu, wu))]
    def wave(t, _):
        for c in range(PH):
            step = t - c

            @pl.when(step == 0)
            def _(c=c):
                begin(c)

            @pl.when(jnp.logical_and(step > 0, step < n))
            def _(c=c, step=step):
                for m in range(SUB):
                    ag(c, m, step - 1).wait_recv()

                    @pl.when(step < n - 1)
                    def _(m=m):
                        ag(c, m, step).start()

                    fw(c, m, step).start()

        @pl.when(t >= n)
        def _():
            ready(t - n)
            shrink_unit(t - n)
            for u in units:
                unit(t - n, *u)

        return 0

    lax.fori_loop(0, n + PH - 1, wave, 0)

    last = PH - 1
    ready(last)
    shrink_unit(last)
    for cp in m_copies:
        cp.wait()
    owned = accs[...] * own_mask[...]
    tall = owned.shape[0] // 2
    packed = (owned[:tall] + owned[tall:]).astype(BF16)
    share = -(-len(units) // stages)
    for b in range(stages):
        ar_out[b] = packed
        cp = pltpu.make_async_remote_copy(
            src_ref=ar_out.at[b], dst_ref=ar_in.at[b], send_sem=ar_send.at[b], recv_sem=ar_recv.at[b],
            device_id=(group, partners[b]), device_id_type=MESH,
        )
        cp.start()
        for u in units[b * share : (b + 1) * share]:
            unit(last, *u)
        cp.wait()
        packed = (ar_out[b].astype(F32) + ar_in[b].astype(F32)).astype(BF16)

    rank = packed.shape[1] // 2
    whole = packed.astype(F32)
    turned = pltpu.roll(whole, rank, 1)
    low = lax.broadcasted_iota(jnp.int32, whole.shape, 1) < rank
    twice = jnp.concatenate([jnp.where(low, whole, turned), jnp.where(low, turned, whole)], axis=0).astype(BF16)

    def drain(ph, _):
        def one(step, _):
            for m in range(SUB):
                fw(ph, m, step).wait_send()
            return 0

        lax.fori_loop(0, n, one, 0)

        def two(step, _):
            for m in range(SUB):
                ag(ph, m, step).wait_send()
            return 0

        lax.fori_loop(0, n - 1, two, 0)
        return 0

    lax.fori_loop(0, PH, drain, 0)

    twice32 = twice.astype(F32)
    pair_of = row_pair[...]
    taken = ex.shape[0] // width
    for k in range(ex.shape[0] // (2 * rank)):
        lo = k * 2 * rank
        x[0, lo // width, :, lo % width : lo % width + 2 * rank] = jnp.where(pair_of == 2.0 * k, twice32, 0.0).astype(BF16)
    for lo, size in spans(ffw, 256):
        gate = accg[:, lo : lo + size]
        up = accu[:, lo : lo + size]
        for k in range(taken):
            up += dot(x[0, k], ex[k * width : (k + 1) * width, lo : lo + size])
        hid[:, lo : lo + size] = (gate / (1.0 + jnp.exp(-gate)) * up).astype(BF16)

    def sx(c):
        return pltpu.make_async_remote_copy(
            src_ref=x.at[1 - core, c], dst_ref=sib.at[c], send_sem=sx_send.at[c], recv_sem=sx_recv.at[c],
            device_id=(group, other), device_id_type=MESH,
        )

    def rs(c, step):
        return pltpu.make_async_remote_copy(
            src_ref=x.at[core, c, rows_of(step + 1), :], dst_ref=ring.at[c, step],
            send_sem=rs_send.at[c, step], recv_sem=rs_recv.at[c, step],
            device_id=(group, nxt), device_id_type=MESH,
        )

    def down(c):
        def fill(h):
            d_copy(h, c).wait()
            for lo, size in spans(width, 256):
                x[h, c, :, lo : lo + size] = dot(hid[...], wd[h, c, :, lo : lo + size]).astype(BF16)

        fill(1 - core)
        sx(c).start()
        fill(core)

    def kick(c):
        sx(c).wait_recv()
        r = rows_of(1)
        x[core, c, r, :] = (x[core, c, r, :].astype(F32) + sib[c, r, :].astype(F32)).astype(BF16)
        rs(c, 0).start()

    def lead(c, _):
        down(c)

        @pl.when(c > 0)
        def _():
            kick(c - 1)

        return 0

    lax.fori_loop(0, PH, lead, 0)
    kick(PH - 1)

    def total(c, step):
        rs(c, step - 1).wait_recv()
        r = rows_of(step + 1)
        return (x[core, c, r, :].astype(F32) + sib[c, r, :].astype(F32) + ring[c, step - 1].astype(F32)).astype(BF16)

    def hop(step, _):
        for c in range(PH):
            x[core, c, rows_of(step + 1), :] = total(c, step)
            rs(c, step).start()
        return 0

    lax.fori_loop(1, n - 1, hop, 0)
    for c in range(PH):
        out[:, c * width : (c + 1) * width] = total(c, n - 1)
    for c in range(PH):
        sx(c).wait_send()

        def three(step, _, c=c):
            rs(c, step).wait_send()
            return 0

        lax.fori_loop(0, n - 1, three, 0)


def local(count, tokens, gate_weight, up_weight, down_weight, adapter_shrink, adapter_expand, adapter_list, block_slot, pool_slot):
    own_rows, model = tokens.shape
    half = model // 2
    width = half // PH
    n = count // 2
    rows = 2 * own_rows
    token_count = n * rows
    rank = adapter_shrink.shape[1]
    ffw = gate_weight.shape[1]
    adapters = adapter_expand.shape[0]
    stages = count.bit_length() - 1
    core = lax.axis_index("tensor") % 2
    swap = [(i, i ^ 1) for i in range(count)]

    kept = lax.dynamic_slice_in_dim(tokens, core * half, half, 1)
    given = lax.dynamic_slice_in_dim(tokens, (1 - core) * half, half, 1)
    got = lax.ppermute(given, "tensor", swap)
    x_in = jnp.where(core == 0, jnp.concatenate([kept, got]), jnp.concatenate([got, kept]))

    dma = pltpu.SemaphoreType.DMA
    flops = 2 * token_count * model * ffw * 3
    reduced = pl.pallas_call(
        functools.partial(kernel, count == 16),
        out_shape=jax.ShapeDtypeStruct((rows, half), BF16),
        in_specs=[pl.BlockSpec(memory_space=pl.ANY)] * 6 + [pl.BlockSpec(memory_space=pltpu.SMEM)] * 3,
        out_specs=pl.BlockSpec(memory_space=pltpu.VMEM),
        scratch_shapes=[
            pltpu.VMEM((2, PH, token_count, width), BF16),
            pltpu.VMEM((2, PH, width, ffw), BF16),
            pltpu.VMEM((2, PH, width, ffw), BF16),
            pltpu.VMEM((2, PH, ffw, width), BF16),
            pltpu.VMEM((2, PH, 2 * rank, width), BF16),
            pltpu.VMEM((adapters * rank, ffw), BF16),
            pltpu.VMEM((token_count, 2 * rank), F32),
            pltpu.VMEM((token_count, 2 * rank), F32),
            pltpu.VMEM((token_count, ffw), F32),
            pltpu.VMEM((token_count, ffw), F32),
            pltpu.VMEM((token_count, 2 * rank), F32),
            pltpu.VMEM((token_count, ffw), BF16),
            pltpu.VMEM((PH, token_count, width), BF16),
            pltpu.VMEM((PH, n - 1, rows, width), BF16),
            pltpu.VMEM((stages, token_count // 2, 2 * rank), BF16),
            pltpu.VMEM((stages, token_count // 2, 2 * rank), BF16),
            dma((PH,)),
            dma((2, 2, PH)),
            dma((2, 2, PH)),
            dma((2, PH)),
            dma((1,)),
            dma((PH, SUB, n - 1)),
            dma((PH, SUB, n - 1)),
            dma((PH, SUB, n)),
            dma((PH, SUB, n)),
            dma((stages,)),
            dma((stages,)),
            dma((PH,)),
            dma((PH,)),
            dma((PH, n - 1)),
            dma((PH, n - 1)),
        ],
        compiler_params=pltpu.CompilerParams(
            collective_id=0, has_side_effects=True, vmem_limit_bytes=63 * 1024 * 1024
        ),
        cost_estimate=pl.CostEstimate(flops=flops, bytes_accessed=6 * model * ffw, transcendentals=token_count * ffw),
    )(
        x_in,
        gate_weight.reshape(2, PH, width, ffw),
        up_weight.reshape(2, PH, width, ffw),
        down_weight,
        adapter_shrink[0],
        adapter_expand.reshape(adapters * rank, ffw),
        adapter_list,
        block_slot,
        pool_slot,
    )
    mine = lax.dynamic_slice_in_dim(reduced, core * own_rows, own_rows, 0)
    theirs = lax.dynamic_slice_in_dim(reduced, (1 - core) * own_rows, own_rows, 0)
    got = lax.ppermute(theirs, "tensor", swap)
    return jnp.where(core == 0, jnp.concatenate([mine, got], 1), jnp.concatenate([got, mine], 1))


def solution(mesh):
    return jax.shard_map(
        functools.partial(local, mesh.shape["tensor"]),
        mesh=mesh,
        in_specs=(
            P(("groups", "tensor"), None),
            P(None, "tensor"),
            P(None, "tensor"),
            P("tensor", None),
            P("tensor", None, None),
            P(None, None, "tensor"),
            P("groups"),
            P("groups"),
            P(),
        ),
        out_specs=P(("groups", "tensor"), None),
        check_vma=False,
    )
```
